256 devices in a mesh: clus: 16 (over x_lo, z), blk: 16 (over x_hi, y, core).
Axes of the slice: x: 4 (x_hi: 2, x_lo: 2; x = x_hi * 2 + x_lo), y: 4, z: 8, core: 2. Of those that a mesh axis runs over, the one named last changes fastest.
Arguments:
- embeddings: bfloat16 [163840, 1024], P(('clus', 'blk')), parts along dimension 0, as said below
- cluster_ids: int32 [163840], P(('clus', 'blk')), parts along dimension 0, may hold values from 0 to 7, never falling along the last dimension, each value on 1 to 5120 neighbouring positions
- valid: int32 [163840], P(('clus', 'blk')), parts along dimension 0, may hold values 0 or 1
Outputs:
- nearest: float32 [163840], P(('clus', 'blk')), parts along dimension 0
The draws below stay inside these ranges and needn't reach their ends.
There are 16 independent parts, one for each index of `clus`. The reference program is written for one: setup_inputs(seed, part) draws one part's arguments, and reference() takes and returns one part's arrays. A program takes and returns all parts, laid end to end along the dimension named above; each array names one. Nothing has to cross between parts.
Inputs may be any that keep to these rules, and one draw needn't show every extreme that they name: Each row of embeddings is finite and not all zero.
All inputs are finite; a program needn't handle non-finite values. No bound on the sum of `valid` on one device may be relied on, other than what follows from the above.
Results may differ from the reference program's by a relative error of at most 0.00039.
Values may be sent and summed in bfloat16 or wider, within the bound.
No kernel may reach another device: no remote copies, remote signals or barrier semaphores. Data moves between devices by JAX's collectives and lax.ppermute only.
A program may use at most 64 MiB of HBM per device.

```python
import math
import jax
import jax.numpy as jnp
import numpy as np
from jax import lax

D = 1024
ROW_DEV = 640
ROWS = 10240


def draw_embeddings(key, part):
    key = jax.random.fold_in(key, 11)
    keys = jax.random.split(key, 4)
    noise = jax.random.normal(keys[0], (ROWS, D), jnp.float32)
    partner = jax.random.permutation(keys[1], ROWS)
    strength = jax.random.uniform(keys[2], (ROWS, 1), jnp.float32, 0.2, 1.5)
    scales = jnp.exp(jax.random.uniform(keys[3], (ROWS, 1), jnp.float32, 0.0, 2.3))
    return (scales * (noise + strength * noise[partner])).astype(jnp.bfloat16)


def plant(drawn, rng, smallest, high):
    dims = drawn.shape
    index_at = [jax.random.randint(jax.random.fold_in(rng, axis), (), 0, dims[axis]) for axis in range(len(dims))]
    drawn = drawn.at[tuple(index_at)].set(smallest)
    longest = dims.index(max(dims))
    index_at[longest] = (index_at[longest] + 1) % dims[longest]
    return drawn.at[tuple(index_at)].set(high)


def split_up(number_of, total, limit, lean):
    weights = [(1 << 20) // math.isqrt(rank ** lean) + 1 for rank in range(2, number_of + 1)]
    spare, counts = total - limit - (number_of - 1), [1] * (number_of - 1)
    while spare > 0:
        free = [i for i in range(number_of - 1) if counts[i] < limit]
        mass, budget = sum([weights[i] for i in free]), spare
        for i in free:
            extra = min(limit - counts[i], max(1, budget * weights[i] // mass), spare)
            counts[i] = counts[i] + extra
            spare = spare - extra
    return np.array([limit] + counts)


def ragged_sizes(stream_key, count, total, bound, slope):
    if count == 2:
        one = jax.random.randint(stream_key, (), max(1, total - bound), min(bound, total - 1) + 1)
        return jnp.stack([one, total - one])
    sizes = jnp.asarray(split_up(count, total, bound, slope), jnp.int32)
    twos = (count - 1) // 2
    source_of, receiver = sizes[1:1 + 2 * twos:2], sizes[2:2 + 2 * twos:2]
    room = jnp.minimum(source_of - 1, bound - receiver)
    passed = jax.random.randint(jax.random.fold_in(stream_key, 1), (twos,), 0, 1 << 20) % (room + 1)
    sizes = sizes.at[1:1 + 2 * twos:2].set(source_of - passed).at[2:2 + 2 * twos:2].set(receiver + passed)
    return sizes[jax.random.permutation(jax.random.fold_in(stream_key, 2), count)]


def setup_inputs(seed: int = 0, part: int = 0) -> dict:
    key_of = jax.random.split(jax.random.key(seed), 4)
    part_splits = jax.random.split(jax.random.fold_in(key_of[3], part), 4)
    return {
        "embeddings": draw_embeddings(jax.random.fold_in(jax.random.fold_in(key_of[3], part), 71), part),
        "cluster_ids": jnp.searchsorted(jnp.cumsum(ragged_sizes(part_splits[1], 8, ROWS, ROWS // 2, 2)), jnp.arange(ROWS), side="right").astype(jnp.int32),
        "valid": plant((jax.random.randint(part_splits[2], (ROWS,), 0, 8) < 7).astype(jnp.int32), jax.random.fold_in(part_splits[2], 1), 0, 1),
    }


def normalize(embeddings):
    values = embeddings.astype(jnp.float32)
    scale = lax.rsqrt(lax.optimization_barrier(jnp.sum(values * values, axis=1)) + 1e-06)
    return (values * scale[:, None]).astype(jnp.bfloat16)

def reference(embeddings, cluster_ids, valid):
    unit = normalize(embeddings)
    label = jnp.where(valid > 0, cluster_ids, -1).astype(jnp.int32)
    positions = jnp.arange(ROWS, dtype=jnp.int32)

    def one_block(index):
        start = (index * ROW_DEV).astype(jnp.int32)
        query = lax.dynamic_slice_in_dim(unit, start, ROW_DEV, 0)
        q_label = lax.dynamic_slice_in_dim(label, start, ROW_DEV, 0)
        q_pos = start + jnp.arange(ROW_DEV, dtype=jnp.int32)
        scores = jnp.dot(query, unit.T, preferred_element_type=jnp.float32)
        match = (q_label[:, None] == label[None, :]) & (q_label[:, None] >= 0) & (q_pos[:, None] != positions[None, :])
        return lax.optimization_barrier(jnp.max(jnp.where(match, scores, -1.0), axis=1))
    blocks = lax.map(one_block, jnp.arange(ROWS // ROW_DEV, dtype=jnp.int32))
    return blocks.reshape(ROWS)
```

```python
import functools

import jax
import jax.numpy as jnp
import numpy as np
from jax import lax
from jax.experimental import pallas as pl
from jax.experimental.pallas import tpu as pltpu
from jax.sharding import PartitionSpec as P

N = 16
PAD = 16

MODE = (1, 0, 0, 0, 2, 3, 1, 2)


def up(chip):
    return chip // 4 * 4 + (chip + 1) % 4


def down(chip):
    return chip // 4 * 4 + (chip + 3) % 4


ALONG = [(2 * c, 2 * up(c)) for c in range(8)] + [(2 * c + 1, 2 * down(c) + 1) for c in range(8)]
PASSES_ON = [MODE[d // 2] >> d % 2 & 1 for d in range(N)]
BUDDY = [(d, d ^ 1) for d in range(N)]
ACROSS = [(d, d ^ 8) for d in range(N)]


def arrived(held, moves):
    got = [-1] * N
    for s, t in moves:
        got[t] = held[s]
    return got


OF = [list(range(N))]
OF.append(arrived(OF[0], BUDDY))
OF.append(arrived(OF[0], ALONG))
OF.append(arrived(OF[2], BUDDY))
OF.append(arrived(OF[0], ACROSS))
OF.append(arrived(OF[4], BUDDY))
OF.append(arrived([OF[2 if PASSES_ON[d] else 1][d] for d in range(N)], ALONG))
LATE = (6, 7)

WORK = (
    [[[(0, 1), (0, 6), (3, 6)], [(1, 8), (6, 8)], [(3, 7), (7, 8)]],
     [[(1, 3)], [(1, 9), (3, 9)], [(1, 2), (2, 9)]],
     [[(0, 2), (2, 3)], [], [(2, 6), (6, 10)]],
     [[(0, 3), (0, 5), (3, 5)], [(3, 11), (5, 11)], [(0, 4), (4, 11)]],
     [[(2, 4), (2, 5), (4, 5)], [(5, 12)], [(3, 4)]],
     [[(2, 7), (5, 7)], [(5, 13), (7, 13)], [(6, 13)]],
     [[(1, 6), (4, 6), (6, 7)], [(6, 14), (7, 14)], [(1, 5), (5, 6)]],
     [[(1, 4), (1, 7), (4, 7)], [(7, 15)], [(0, 7)]],
     [[(8, 11), (8, 14), (11, 14)], [(0, 8)], [(8, 15), (11, 15)]],
     [[(8, 9), (9, 11), (9, 14)], [], [(9, 13), (13, 14)]],
     [[(8, 10)], [(2, 8), (2, 10)], [(9, 10)]],
     [[(8, 13), (10, 11), (11, 13)], [(3, 8), (3, 10)], [(8, 12), (11, 12)]],
     [[(10, 12), (12, 13)], [(4, 10), (4, 12)], [(4, 8), (5, 8)]],
     [[(10, 13), (10, 15), (13, 15)], [(5, 10)], [(4, 9), (5, 9)]],
     [[(9, 12), (12, 14), (14, 15)], [(6, 9), (6, 12)], [(7, 10), (10, 14)]],
     [[(9, 15), (12, 15), (14, 15)], [(7, 9), (7, 12)], [(6, 11), (7, 11)]]])

BACK = (
    (),
    (
        (1, -1, 0, -1, 5, 2, 7, 4, -1, 11, 8, 3, 13, 10, 6, 9),
        (6, -1, 3, 5, -1, 7, 4, -1, 0, 8, -1, 13, 10, 15, 9, 12),
    ),
    (
        (3, 9, 10, 0, 12, -1, 14, 1, 11, 13, 2, 8, 5, 4, 7, 6),
        (8, 2, 6, 11, 3, 13, 1, 0, 15, 14, 9, 10, 4, 5, 12, 7),
        (7, 3, -1, 4, 2, 6, 5, 15, 14, -1, -1, 12, 8, 9, 10, 11),
    ),
)


def check():
    served = set()
    for d in range(N):
        for stage, pairs in enumerate(WORK[d]):
            for a, b in pairs:
                for owner, partner in ((a, b), (b, a)):
                    if owner == d or any(row[d] == owner for later in BACK[stage:] for row in later):
                        served.add((owner, partner))
    assert all((a, b) in served for a in range(N) for b in range(N) if 0 < abs(a - b) <= 8)


check()


def full(row):
    free = [t for t in range(N) if t not in row]
    return [(d, t if t >= 0 else free.pop()) for d, t in enumerate(row)]


def grouped(pairs, lead):
    left, order = list(pairs), []
    while left:
        if not any(lead in p for p in left):
            lead = max(range(N), key=lambda b: sum(b in p for p in left))
        group = [p for p in left if lead in p]
        order += [(lead, p[0] + p[1] - lead) for p in group]
        left = [p for p in left if lead not in p]
    return order


FIELDS = 5
LATER = 6
COST = (0, 2 * 10 ** 10, 0)


def first_schedule():
    longest = max(len(WORK[d][0]) for d in range(N))
    use = np.zeros((N, 4), np.int32)
    pairs = np.full((N, longest * FIELDS), -1, np.int32)
    for d in range(N):
        slot = {OF[s][d]: s for s in reversed(range(4))}
        order = grouped(WORK[d][0], d)
        for k, (a, b) in enumerate(order):
            use[d, slot[a]] |= 1
            use[d, slot[b]] |= 2
            end = k + 1 == len(order) or order[k + 1][0] != a
            pairs[d, FIELDS * k:FIELDS * (k + 1)] = slot[a], slot[b], a, b, end
        use[d, 0] = 3
        for stage, lead in ((1, 4), (2, 6)):
            for pair in WORK[d][stage]:
                for b in pair:
                    if b != OF[lead][d] and b in slot:
                        use[d, slot[b]] |= 2
    return use, pairs


def late_schedule(stage, lead):
    early = np.zeros((N, 2 + 2 * LATER), np.int32)
    other = np.zeros((N, 4), np.int32)
    for d in range(N):
        own = OF[lead][d]
        slot = {OF[s][d]: s for s in reversed(range(lead))}
        partners = [p[0] + p[1] - own for p in WORK[d][stage]]
        assert all(own in p for p in WORK[d][stage])
        near = [b for b in partners if slot[b] < 4]
        early[d, :2] = own, len(near)
        for k, b in enumerate(near):
            early[d, 2 + 2 * k:4 + 2 * k] = slot[b], b
        for b in partners:
            if slot[b] >= 4:
                assert not other[d, slot[b] - 4]
                other[d, slot[b] - 4], other[d, slot[b] - 2] = 1, b
    return early, other


def pack_kernel(ids_in, valid_in, rows_in, out, out_x, ids, valid, raw, unit, in_sems, out_sems):
    rows, depth = raw.shape
    parts = [pl.ds(at, 128) for at in range(0, rows, 128)]
    tail = pl.ds(rows, 2 * PAD)
    loads = [pltpu.make_async_copy(rows_in.at[p], raw.at[p], in_sems.at[k]) for k, p in enumerate(parts)]
    small = [pltpu.make_async_copy(ids_in, ids, in_sems.at[len(parts)]),
             pltpu.make_async_copy(valid_in, valid, in_sems.at[len(parts) + 1])]
    ends = parts + [pl.ds(rows, PAD)], parts + [tail]
    stores = [[pltpu.make_async_copy(unit.at[p], ref.at[p], out_sems.at[n, k]) for n, (ref, p) in enumerate(zip((out, out_x), both))]
              for k, both in enumerate(zip(*ends))]
    for load in loads[:1] + small + loads[1:]:
        load.start()
    for k, (load, part) in enumerate(zip(loads, parts)):
        load.wait()
        values = raw[part, :].astype(jnp.float32)
        scale = lax.rsqrt(jnp.sum(values * values, axis=1, keepdims=True) + 1e-06)
        unit[part, :] = (values * scale).astype(jnp.bfloat16)
        [store.start() for store in stores[k]]
        if k == 0:
            for load in small:
                load.wait()
            label = jnp.where(valid[...] > 0, ids[...], -1).astype(jnp.float32).reshape(1, rows)
            label = jnp.concatenate([label, jnp.zeros((1, depth - rows), jnp.float32)], axis=1)
            unit[tail, :] = jnp.broadcast_to(label, (2 * PAD, depth)).astype(jnp.bfloat16)
            [store.start() for store in stores[-1]]
    for store in sum(stores, []):
        store.wait()


def pack(embeddings, cluster_ids, valid):
    rows, depth = embeddings.shape
    anywhere = pl.BlockSpec(memory_space=pl.ANY)
    return pl.pallas_call(
        pack_kernel,
        out_shape=[jax.ShapeDtypeStruct((rows + n * PAD, depth), jnp.bfloat16) for n in (1, 2)],
        in_specs=[anywhere] * 3,
        out_specs=[anywhere] * 2,
        scratch_shapes=[
            pltpu.VMEM((rows,), jnp.int32),
            pltpu.VMEM((rows,), jnp.int32),
            pltpu.VMEM((rows, depth), jnp.bfloat16),
            pltpu.VMEM((rows + 2 * PAD, depth), jnp.bfloat16),
            pltpu.SemaphoreType.DMA((rows // 128 + 2,)),
            pltpu.SemaphoreType.DMA((2, rows // 128 + 1)),
        ],
        compiler_params=pltpu.CompilerParams(vmem_limit_bytes=58 * 2 ** 20),
        cost_estimate=pl.CostEstimate(flops=4 * rows * depth, bytes_accessed=4 * rows * depth, transcendentals=rows),
    )(cluster_ids, valid, embeddings)


def turn(block, to):
    rows = to.shape[1]

    def part(k, _):
        at = pl.ds(pl.multiple_of(k * 128, 128), 128)
        to[:, at] = jnp.transpose(block[at, :])
        return 0

    lax.fori_loop(0, rows // 128, part, 0)


def row_labels(block, rows):
    label = block[rows:rows + PAD, :rows].astype(jnp.float32)
    return jnp.transpose(jnp.broadcast_to(label[:1], (128, rows)))


def column_labels(block, rows):
    label = block[rows:rows + PAD, :rows].astype(jnp.float32)[:8]
    return jnp.where(label < 0.0, -2.0, label)


def tile(left, right, labels, keys, racc, out, b, own):
    rows, wide, step = racc.shape[0], 256, 64
    for at in range(0, rows, wide):
        lanes = [slice(c, c + 128) for c in range(0, min(wide, rows - at), 128)]
        scores = jnp.dot(left, right[:, at:at + 128 * len(lanes)], preferred_element_type=jnp.float32)
        key = [keys[:, at + c.start:at + c.stop][None] for c in lanes]
        low = [jnp.full((8, 128), -1.0, jnp.float32) for _ in lanes]
        for r in range(0, rows, step):
            label = labels[r:r + step, :].reshape(step // 8, 8, 128)
            high = racc[r:r + step, :].reshape(step // 8, 8, 128)
            for n, c in enumerate(lanes):
                match = label == key[n]
                if own:
                    row = r + 8 * lax.broadcasted_iota(jnp.int32, (step // 8, 8, 128), 0) + (
                        lax.broadcasted_iota(jnp.int32, (step // 8, 8, 128), 1))
                    col = lax.broadcasted_iota(jnp.int32, (step // 8, 8, 128), 2) + (at + c.start)
                    match = match & (row != col)
                part = jnp.where(match, scores[r:r + step, c].reshape(step // 8, 8, 128), -1.0)
                high = jnp.maximum(high, part)
                if not own:
                    low[n] = jnp.maximum(low[n], jnp.max(part, axis=0))
            racc[r:r + step, :] = high.reshape(step, 128)
        if not own:
            for n, c in enumerate(lanes):
                cols = slice(at + c.start, at + c.stop)
                out[b, :, cols] = jnp.maximum(out[b, :, cols], jnp.max(low[n], axis=0, keepdims=True))


def flush(racc, out, a):
    most = jnp.max(jnp.transpose(racc[...]), axis=0, keepdims=True)
    out[a] = jnp.maximum(out[a], most)
    racc[...] = jnp.full_like(racc, -1.0)


def give(out, back, results):
    me = lax.axis_index("blk")
    for k, result in enumerate(results):
        to = back[me, k]
        result[...] = jnp.where(to >= 0, out[jnp.maximum(to, 0)], -1.0)


def first_kernel(count, returns, use, pairs, back, *refs):
    blocks, (out, turned, lkey), results = refs[:4], refs[4:7], refs[7:7 + returns]
    unit, lcol, racc = refs[7 + returns:]
    rows = racc.shape[0]
    me = lax.axis_index("blk")
    out[...] = jnp.full_like(out, -1.0)
    racc[...] = jnp.full_like(racc, -1.0)
    for s, block in enumerate(blocks):
        lkey[s] = column_labels(block, rows)

        @pl.when((use[me, s] & 1) > 0)
        def _(s=s, block=block):
            def fetch(k, _):
                at = pl.ds(pl.multiple_of(k * 128, 128), 128)
                unit[s, at, :] = block[at, :]
                return 0

            lax.fori_loop(0, rows // 128, fetch, 0)
            lcol[s] = row_labels(block, rows)

        @pl.when((use[me, s] & 2) > 0)
        def _(s=s, block=block):
            turn(block, turned.at[s])

    tile(unit[0], turned.at[0], lcol.at[0], lkey.at[0], racc, out, None, True)

    @pl.when(pairs[me, 0] != 0)
    def _():
        flush(racc, out, me)

    def each(k, _):
        i, j, a, b, end = [pairs[me, FIELDS * k + n] for n in range(FIELDS)]

        @pl.when(i >= 0)
        def _():
            tile(unit[i], turned.at[j], lcol.at[i], lkey.at[j], racc, out, b, False)

            @pl.when(end > 0)
            def _():
                flush(racc, out, a)

        return 0

    lax.fori_loop(0, count, each, 0)
    give(out, back, results)


def with_early(me, early, block, turned, lkey, lcol, racc, out):
    rows = racc.shape[0]
    lcol[...] = row_labels(block, rows)
    racc[...] = jnp.full_like(racc, -1.0)

    def each(k, _):
        j, b = early[me, 2 + 2 * k], early[me, 3 + 2 * k]
        tile(block[:rows, :], turned.at[j], lcol, lkey.at[j], racc, out, b, False)
        return 0

    lax.fori_loop(0, early[me, 1], each, 0)


def second_kernel(returns, early, meets, back, far, turned, lkey, before, out, far_turned, *refs):
    results, (lcol, racc) = refs[:returns], refs[returns:]
    me = lax.axis_index("blk")
    out[...] = before[...]
    with_early(me, early, far, turned, lkey, lcol, racc, out)

    @pl.when(early[me, 1] > 0)
    def _():
        flush(racc, out, early[me, 0])

    @pl.when(meets[me, 0] > 0)
    def _():
        turn(far, far_turned)

    give(out, back, results)


def last_kernel(returns, early, meets, back, block, far, far_other, turned, far_turned, lkey, before, mine, *refs):
    results, (out, lcol, racc, other_turned, fkey) = refs[:returns], refs[returns:]
    rows = racc.shape[0]
    me = lax.axis_index("blk")
    out[...] = before[...]
    with_early(me, early, block, turned, lkey, lcol, racc, out)

    @pl.when(meets[me, 0] > 0)
    def _():
        fkey[...] = column_labels(far, rows)
        tile(block[:rows, :], far_turned, lcol, fkey, racc, out, meets[me, 2], False)

    @pl.when(meets[me, 1] > 0)
    def _():
        fkey[...] = column_labels(far_other, rows)
        turn(far_other, other_turned)
        tile(block[:rows, :], other_turned, lcol, fkey, racc, out, meets[me, 3], False)

    flush(racc, out, early[me, 0])
    mine[...] = out[me]
    give(out, back, results)


def run(stage, kernel, tables, operands, out_shape, scratch):
    vmem = pl.BlockSpec(memory_space=pltpu.VMEM)
    smem = pl.BlockSpec(memory_space=pltpu.SMEM)
    rows = out_shape[0].shape[-1]
    one = jax.ShapeDtypeStruct((1, rows), jnp.float32)
    returns = len(BACK[stage])
    tables = [jnp.asarray(t) for t in (*tables, np.array(BACK[stage] + ((0,) * N,), np.int32).T)]
    out_shape = out_shape + [one] * returns
    got = pl.pallas_call(
        functools.partial(kernel, returns),
        out_shape=out_shape,
        in_specs=[smem] * 3 + [vmem] * len(operands),
        out_specs=[vmem] * len(out_shape),
        scratch_shapes=scratch,
        compiler_params=pltpu.CompilerParams(vmem_limit_bytes=20 * 2 ** 20),
        cost_estimate=pl.CostEstimate(flops=COST[stage], bytes_accessed=0, transcendentals=0),
    )(*tables, *operands)
    return got[:len(got) - returns], got[len(got) - returns:]


def shards(embeddings, cluster_ids, valid):
    me = lax.axis_index("blk")
    move = functools.partial(lax.ppermute, axis_name="blk")
    mine, mine_x = pack(embeddings, cluster_ids, valid)
    near = move(mine, perm=ALONG)
    far = move(mine_x, perm=ACROSS)
    other = move(mine, perm=BUDDY)
    second = move(jnp.where((sum(p << d for d, p in enumerate(PASSES_ON)) >> me) & 1 > 0, near, other), perm=ALONG)
    near_other = move(near, perm=BUDDY)
    blocks = [mine, other, near, near_other]
    rows, depth = embeddings.shape
    maxima = jax.ShapeDtypeStruct((N, 1, rows), jnp.float32)
    one = jax.ShapeDtypeStruct((1, rows), jnp.float32)
    turned = jax.ShapeDtypeStruct((depth, rows), jnp.bfloat16)
    by_row = pltpu.VMEM((rows, 128), jnp.float32)
    use, pairs = first_schedule()
    (got, early, keys), back = run(
        0, functools.partial(first_kernel, pairs.shape[1] // FIELDS), (use, pairs), blocks,
        [maxima, jax.ShapeDtypeStruct((4, depth, rows), jnp.bfloat16), jax.ShapeDtypeStruct((4, 8, rows), jnp.float32)],
        [pltpu.VMEM((4, rows, depth), jnp.bfloat16), pltpu.VMEM((4, rows, 128), jnp.float32), by_row])
    far, got = lax.optimization_barrier((far, got))
    far_other = move(far, perm=[(d, t) for d, t in BUDDY if d // 2 in LATE])
    (got, far_turned), more = run(
        1, second_kernel, (late_schedule(1, 4)[0], late_schedule(2, 6)[1]), [far, early, keys, got],
        [maxima, turned], [by_row, by_row])
    second, got = lax.optimization_barrier((second, got))
    (result,), last = run(
        2, last_kernel, late_schedule(2, 6), [second, far, far_other, early, far_turned, keys, got],
        [one], [pltpu.VMEM(maxima.shape, jnp.float32), by_row, by_row,
                pltpu.VMEM(turned.shape, jnp.bfloat16), pltpu.VMEM((8, rows), jnp.float32)])
    for rows, row in zip([*back, *more, *last], sum(BACK, ())):
        result = jnp.maximum(result, move(rows, perm=full(row)))
    return result.reshape(-1)


def solution(mesh):
    return jax.shard_map(
        shards,
        mesh=mesh,
        in_specs=(P(("clus", "blk"), None), P(("clus", "blk")), P(("clus", "blk"))),
        out_specs=P(("clus", "blk")),
        check_vma=False,
    )
```

```python
import functools

import jax
import jax.numpy as jnp
import numpy as np
from jax import lax
from jax.experimental import pallas as pl
from jax.experimental.pallas import tpu as pltpu
from jax.sharding import PartitionSpec as P

N = 16
PAD = 16

MODE = (3, 0, 0, 0, 3, 3, 1, 2)


def up(chip):
    return chip // 4 * 4 + (chip + 1) % 4


def down(chip):
    return chip // 4 * 4 + (chip + 3) % 4


ALONG = [(2 * c, 2 * up(c)) for c in range(8)] + [(2 * c + 1, 2 * down(c) + 1) for c in range(8)]
PASSES_ON = [MODE[d // 2] >> d % 2 & 1 for d in range(N)]
BUDDY = [(d, d ^ 1) for d in range(N)]
ACROSS = [(d, d ^ 8) for d in range(N)]


def arrived(held, moves):
    got = [-1] * N
    for s, t in moves:
        got[t] = held[s]
    return got


OF = [list(range(N))]
OF.append(arrived(OF[0], BUDDY))
OF.append(arrived(OF[0], ALONG))
OF.append(arrived(OF[2], BUDDY))
OF.append(arrived(OF[0], ACROSS))
OF.append(arrived(OF[4], BUDDY))
OF.append(arrived([OF[2 if PASSES_ON[d] else 1][d] for d in range(N)], ALONG))
LATE = (6, 7)

WORK = (
    [[[(1, 3)], [(1, 8), (6, 8)], [(0, 7), (7, 8)]],
     [[(0, 1), (0, 6), (3, 6)], [(3, 9), (6, 9)], [(1, 2), (2, 9)]],
     [[(0, 2), (2, 5), (3, 5)], [], [(6, 10)]],
     [[(0, 3), (0, 5), (2, 3)], [(3, 11), (5, 11)], [(0, 4), (4, 11)]],
     [[(2, 4), (2, 7), (5, 7)], [(7, 12)], [(3, 4), (3, 7)]],
     [[(4, 5), (4, 7)], [(5, 13), (7, 13)], [(2, 6), (6, 13)]],
     [[(1, 4), (4, 6), (6, 7)], [], [(1, 5), (5, 6)]],
     [[(1, 6), (1, 7)], [(7, 15)], []],
     [[(8, 11), (8, 14), (11, 14)], [(0, 8)], [(8, 15), (11, 15)]],
     [[(8, 9), (9, 11), (9, 14)], [(1, 9)], [(9, 13), (13, 14)]],
     [[(8, 13), (11, 13)], [(2, 8), (2, 10)], [(10, 14)]],
     [[(8, 10), (10, 11), (10, 13)], [(3, 8), (3, 10)], [(8, 12), (11, 12)]],
     [[(12, 13), (12, 15), (13, 15)], [(4, 10), (4, 12)], [(4, 8), (5, 8)]],
     [[(10, 12), (10, 15)], [(5, 10), (5, 12)], [(4, 9), (5, 9)]],
     [[(9, 12)], [(6, 12), (6, 14)], [(7, 10), (9, 10)]],
     [[(9, 15), (12, 14), (14, 15)], [(7, 9), (7, 14)], [(6, 11), (7, 11)]]])

BACK = (
    (4, 5, -1, 0, 6, 7, 2, 3),
    (1, 0, 3, 2, 5, 6, 7, 4),
    (3, 2, 6, 7, 0, 1, 4, 5),
    (-1, 3, 1, -1, 7, 4, 5, 6),
)


def check():
    served = set()
    for d in range(N):
        for a, b in sum(WORK[d], []):
            for owner, partner in ((a, b), (b, a)):
                if owner // 2 == d // 2 or any(row[d // 2] == owner // 2 for row in BACK):
                    served.add((owner, partner))
    assert all((a, b) in served for a in range(N) for b in range(N) if 0 < abs(a - b) <= 8)


check()


def sends(pair):
    moves = []
    for core, row in enumerate(pair):
        free = [t for t in range(N // 2) if t not in row]
        moves += [(2 * c + core, 2 * (t if t >= 0 else free.pop()) + core) for c, t in enumerate(row)]
    return moves


def grouped(pairs, lead):
    left, order = list(pairs), []
    while left:
        if not any(lead in p for p in left):
            lead = max(range(N), key=lambda b: sum(b in p for p in left))
        group = [p for p in left if lead in p]
        order += [(lead, p[0] + p[1] - lead) for p in group]
        left = [p for p in left if lead not in p]
    return order


FIELDS = 5
LATER = 6


def first_schedule():
    longest = max(len(WORK[d][0]) for d in range(N))
    use = np.zeros((N, 4), np.int32)
    pairs = np.full((N, longest * FIELDS), -1, np.int32)
    for d in range(N):
        slot = {OF[s][d]: s for s in reversed(range(4))}
        order = grouped(WORK[d][0], d)
        for k, (a, b) in enumerate(order):
            use[d, slot[a]] |= 1
            use[d, slot[b]] |= 2
            end = k + 1 == len(order) or order[k + 1][0] != a
            pairs[d, FIELDS * k:FIELDS * (k + 1)] = slot[a], slot[b], a, b, end
        use[d, 0] = 3
        for stage, lead in ((1, 4), (2, 6)):
            for pair in WORK[d][stage]:
                for b in pair:
                    if b != OF[lead][d] and b in slot:
                        use[d, slot[b]] |= 2
    return use, pairs


def late_schedule(stage, lead):
    early = np.zeros((N, 2 + 2 * LATER), np.int32)
    other = np.zeros((N, 4), np.int32)
    for d in range(N):
        own = OF[lead][d]
        slot = {OF[s][d]: s for s in reversed(range(lead))}
        partners = [p[0] + p[1] - own for p in WORK[d][stage]]
        assert all(own in p for p in WORK[d][stage])
        near = [b for b in partners if slot[b] < 4]
        early[d, :2] = own, len(near)
        for k, b in enumerate(near):
            early[d, 2 + 2 * k:4 + 2 * k] = slot[b], b
        for b in partners:
            if slot[b] >= 4:
                assert not other[d, slot[b] - 4]
                other[d, slot[b] - 4], other[d, slot[b] - 2] = 1, b
    return early, other


def pack_kernel(ids_in, valid_in, rows_in, out, out_x, ids, valid, raw, unit, in_sems, out_sems):
    rows, depth = raw.shape
    parts = [pl.ds(at, 128) for at in range(0, rows, 128)]
    tail = pl.ds(rows, 2 * PAD)
    loads = [pltpu.make_async_copy(rows_in.at[p], raw.at[p], in_sems.at[k]) for k, p in enumerate(parts)]
    small = [pltpu.make_async_copy(ids_in, ids, in_sems.at[len(parts)]),
             pltpu.make_async_copy(valid_in, valid, in_sems.at[len(parts) + 1])]
    ends = parts + [pl.ds(rows, PAD)], parts + [tail]
    stores = [[pltpu.make_async_copy(unit.at[p], ref.at[p], out_sems.at[n, k]) for n, (ref, p) in enumerate(zip((out, out_x), both))]
              for k, both in enumerate(zip(*ends))]
    for load in loads[:1] + small + loads[1:]:
        load.start()
    for k, (load, part) in enumerate(zip(loads, parts)):
        load.wait()
        values = raw[part, :].astype(jnp.float32)
        scale = lax.rsqrt(jnp.sum(values * values, axis=1, keepdims=True) + 1e-06)
        unit[part, :] = (values * scale).astype(jnp.bfloat16)
        [store.start() for store in stores[k]]
        if k == 0:
            for load in small:
                load.wait()
            label = jnp.where(valid[...] > 0, ids[...], -1).astype(jnp.float32).reshape(1, rows)
            label = jnp.concatenate([label, jnp.zeros((1, depth - rows), jnp.float32)], axis=1)
            unit[tail, :] = jnp.broadcast_to(label, (2 * PAD, depth)).astype(jnp.bfloat16)
            [store.start() for store in stores[-1]]
    for store in sum(stores, []):
        store.wait()


def pack(embeddings, cluster_ids, valid):
    rows, depth = embeddings.shape
    anywhere = pl.BlockSpec(memory_space=pl.ANY)
    return pl.pallas_call(
        pack_kernel,
        out_shape=[jax.ShapeDtypeStruct((rows + n * PAD, depth), jnp.bfloat16) for n in (1, 2)],
        in_specs=[anywhere] * 3,
        out_specs=[anywhere] * 2,
        scratch_shapes=[
            pltpu.VMEM((rows,), jnp.int32),
            pltpu.VMEM((rows,), jnp.int32),
            pltpu.VMEM((rows, depth), jnp.bfloat16),
            pltpu.VMEM((rows + 2 * PAD, depth), jnp.bfloat16),
            pltpu.SemaphoreType.DMA((rows // 128 + 2,)),
            pltpu.SemaphoreType.DMA((2, rows // 128 + 1)),
        ],
        compiler_params=pltpu.CompilerParams(vmem_limit_bytes=58 * 2 ** 20),
        cost_estimate=pl.CostEstimate(flops=4 * rows * depth, bytes_accessed=4 * rows * depth, transcendentals=rows),
    )(cluster_ids, valid, embeddings)


def turn(block, to):
    rows = to.shape[1]

    def part(k, _):
        at = pl.ds(pl.multiple_of(k * 128, 128), 128)
        to[:, at] = jnp.transpose(block[at, :])
        return 0

    lax.fori_loop(0, rows // 128, part, 0)


def row_labels(block, rows):
    label = block[rows:rows + PAD, :rows].astype(jnp.float32)
    return jnp.transpose(jnp.broadcast_to(label[:1], (128, rows)))


def column_labels(block, rows):
    label = block[rows:rows + PAD, :rows].astype(jnp.float32)[:8]
    return jnp.where(label < 0.0, -2.0, label)


def tile(left, right, labels, keys, racc, out, b, own):
    rows, wide, step = racc.shape[0], 256, 64
    for at in range(0, rows, wide):
        lanes = [slice(c, c + 128) for c in range(0, min(wide, rows - at), 128)]
        scores = jnp.dot(left, right[:, at:at + 128 * len(lanes)], preferred_element_type=jnp.float32)
        key = [keys[:, at + c.start:at + c.stop][None] for c in lanes]
        low = [jnp.full((8, 128), -1.0, jnp.float32) for _ in lanes]
        for r in range(0, rows, step):
            label = labels[r:r + step, :].reshape(step // 8, 8, 128)
            high = racc[r:r + step, :].reshape(step // 8, 8, 128)
            for n, c in enumerate(lanes):
                match = label == key[n]
                if own:
                    row = r + 8 * lax.broadcasted_iota(jnp.int32, (step // 8, 8, 128), 0) + (
                        lax.broadcasted_iota(jnp.int32, (step // 8, 8, 128), 1))
                    col = lax.broadcasted_iota(jnp.int32, (step // 8, 8, 128), 2) + (at + c.start)
                    match = match & (row != col)
                part = jnp.where(match, scores[r:r + step, c].reshape(step // 8, 8, 128), -1.0)
                high = jnp.maximum(high, part)
                if not own:
                    low[n] = jnp.maximum(low[n], jnp.max(part, axis=0))
            racc[r:r + step, :] = high.reshape(step, 128)
        if not own:
            for n, c in enumerate(lanes):
                cols = slice(at + c.start, at + c.stop)
                out[b, :, cols] = jnp.maximum(out[b, :, cols], jnp.max(low[n], axis=0, keepdims=True))


def flush(racc, out, a):
    most = jnp.max(jnp.transpose(racc[...]), axis=0, keepdims=True)
    out[a] = jnp.maximum(out[a], most)
    racc[...] = jnp.full_like(racc, -1.0)


def merge_kernel(targets, out, other, mine, *sent):
    me = lax.axis_index("blk")
    for n in (0, 1):
        at = me // 2 * 2 + n
        mine[n] = jnp.maximum(out[at], other[at])
        for k, ref in enumerate(sent):
            to = targets[me, k]
            at = jnp.maximum(to, 0) * 2 + n
            ref[n] = jnp.where(to >= 0, jnp.maximum(out[at], other[at]), -1.0)


def split_kernel(*refs):
    *found, keep, pass_on = refs
    core = lax.axis_index("blk") % 2
    for ref, at in ((keep, core), (pass_on, 1 - core)):
        ref[...] = functools.reduce(jnp.maximum, [f[at] for f in found])


def first_kernel(count, use, pairs, *refs):
    blocks, (out, turned, lkey), (unit, lcol, racc) = refs[:4], refs[4:7], refs[7:]
    rows = racc.shape[0]
    me = lax.axis_index("blk")
    out[...] = jnp.full_like(out, -1.0)
    racc[...] = jnp.full_like(racc, -1.0)
    for s, block in enumerate(blocks):
        lkey[s] = column_labels(block, rows)

        @pl.when((use[me, s] & 1) > 0)
        def _(s=s, block=block):
            def fetch(k, _):
                at = pl.ds(pl.multiple_of(k * 128, 128), 128)
                unit[s, at, :] = block[at, :]
                return 0

            lax.fori_loop(0, rows // 128, fetch, 0)
            lcol[s] = row_labels(block, rows)

        @pl.when((use[me, s] & 2) > 0)
        def _(s=s, block=block):
            turn(block, turned.at[s])

    tile(unit[0], turned.at[0], lcol.at[0], lkey.at[0], racc, out, None, True)

    @pl.when(pairs[me, 0] != 0)
    def _():
        flush(racc, out, me)

    def each(k, _):
        i, j, a, b, end = [pairs[me, FIELDS * k + n] for n in range(FIELDS)]

        @pl.when(i >= 0)
        def _():
            tile(unit[i], turned.at[j], lcol.at[i], lkey.at[j], racc, out, b, False)

            @pl.when(end > 0)
            def _():
                flush(racc, out, a)

        return 0

    lax.fori_loop(0, count, each, 0)


def with_early(me, early, block, turned, lkey, lcol, racc, out):
    rows = racc.shape[0]
    lcol[...] = row_labels(block, rows)
    racc[...] = jnp.full_like(racc, -1.0)

    def each(k, _):
        j, b = early[me, 2 + 2 * k], early[me, 3 + 2 * k]
        tile(block[:rows, :], turned.at[j], lcol, lkey.at[j], racc, out, b, False)
        return 0

    lax.fori_loop(0, early[me, 1], each, 0)


def second_kernel(early, meets, far, turned, lkey, before, out, far_turned, fkey, lcol, racc):
    me = lax.axis_index("blk")
    out[...] = before[...]
    with_early(me, early, far, turned, lkey, lcol, racc, out)

    @pl.when(early[me, 1] > 0)
    def _():
        flush(racc, out, early[me, 0])

    @pl.when(meets[me, 0] > 0)
    def _():
        fkey[...] = column_labels(far, racc.shape[0])
        turn(far, far_turned)


def last_kernel(early, meets, block, far_other, turned, far_turned, fkey, lkey, before, out, lcol, racc, other_turned, okey):
    rows = racc.shape[0]
    me = lax.axis_index("blk")
    out[...] = before[...]
    with_early(me, early, block, turned, lkey, lcol, racc, out)

    @pl.when(meets[me, 0] > 0)
    def _():
        tile(block[:rows, :], far_turned, lcol, fkey, racc, out, meets[me, 2], False)

    @pl.when(meets[me, 1] > 0)
    def _():
        okey[...] = column_labels(far_other, rows)
        turn(far_other, other_turned)
        tile(block[:rows, :], other_turned, lcol, okey, racc, out, meets[me, 3], False)

    flush(racc, out, early[me, 0])


def run(kernel, tables, operands, out_shape, scratch=(), flops=0):
    vmem = pl.BlockSpec(memory_space=pltpu.VMEM)
    smem = pl.BlockSpec(memory_space=pltpu.SMEM)
    return pl.pallas_call(
        kernel,
        out_shape=out_shape,
        in_specs=[smem] * len(tables) + [vmem] * len(operands),
        out_specs=[vmem] * len(out_shape),
        scratch_shapes=list(scratch),
        compiler_params=pltpu.CompilerParams(vmem_limit_bytes=12 * 2 ** 20),
        cost_estimate=pl.CostEstimate(flops=flops, bytes_accessed=0, transcendentals=0),
    )(*[jnp.asarray(t) for t in tables], *operands)


def shards(embeddings, cluster_ids, valid):
    me = lax.axis_index("blk")
    move = functools.partial(lax.ppermute, axis_name="blk")
    mine, mine_x = pack(embeddings, cluster_ids, valid)
    near = move(mine, perm=ALONG)
    far = move(mine_x, perm=ACROSS)
    other = move(mine, perm=BUDDY)
    second = move(jnp.where((sum(p << d for d, p in enumerate(PASSES_ON)) >> me) & 1 > 0, near, other), perm=ALONG)
    near_other = move(near, perm=BUDDY)
    blocks = [mine, other, near, near_other]
    rows, depth = embeddings.shape
    maxima = jax.ShapeDtypeStruct((N, 1, rows), jnp.float32)
    one = jax.ShapeDtypeStruct((1, rows), jnp.float32)
    turned = jax.ShapeDtypeStruct((depth, rows), jnp.bfloat16)
    by_row = pltpu.VMEM((rows, 128), jnp.float32)
    use, pairs = first_schedule()
    got, early, keys = run(
        functools.partial(first_kernel, pairs.shape[1] // FIELDS), (use, pairs), blocks,
        [maxima, jax.ShapeDtypeStruct((4, depth, rows), jnp.bfloat16), jax.ShapeDtypeStruct((4, 8, rows), jnp.float32)],
        [pltpu.VMEM((4, rows, depth), jnp.bfloat16), pltpu.VMEM((4, rows, 128), jnp.float32), by_row])
    far, got = lax.optimization_barrier((far, got))
    far_other = move(far, perm=[(d, t) for d, t in BUDDY if d // 2 in LATE])
    got, far_turned, far_keys = run(
        second_kernel, (late_schedule(1, 4)[0], late_schedule(2, 6)[1]), [far, early, keys, got],
        [maxima, turned, jax.ShapeDtypeStruct((8, rows), jnp.float32)], [by_row, by_row], flops=2 * 10 ** 10)
    second, got = lax.optimization_barrier((second, got))
    got, = run(
        last_kernel, late_schedule(2, 6), [second, far_other, early, far_turned, far_keys, keys, got],
        [maxima], [by_row, by_row, pltpu.VMEM(turned.shape, jnp.bfloat16), pltpu.VMEM((8, rows), jnp.float32)])
    targets = np.array([[row[d // 2] for row in BACK[d % 2::2]] for d in range(N)], np.int32)
    two = jax.ShapeDtypeStruct((2, 1, rows), jnp.float32)
    mine, *sent = run(merge_kernel, (targets,), [got, move(got, perm=BUDDY)], [two] * (1 + len(BACK) // 2))
    found = [mine] + [move(s, perm=sends(BACK[2 * k:2 * k + 2])) for k, s in enumerate(sent)]
    keep, pass_on = run(split_kernel, (), found, [one] * 2)
    return jnp.maximum(keep, move(pass_on, perm=BUDDY)).reshape(-1)


def solution(mesh):
    return jax.shard_map(
        shards,
        mesh=mesh,
        in_specs=(P(("clus", "blk"), None), P(("clus", "blk")), P(("clus", "blk"))),
        out_specs=P(("clus", "blk")),
        check_vma=False,
    )
```
